32 devices in a mesh: groups: 1, expert: 8 (over y, x, core), tensor: 4 (over z).
Axes of the slice: x: 2, y: 2, z: 4, core: 2. Of those that a mesh axis runs over, the one named last changes fastest.
Arguments:
- attn_partial: bfloat16 [4, 512, 4096], P('tensor', ('groups', 'expert')), may hold values from -6 to 6
- residual: bfloat16 [512, 4096], P(('groups', 'expert', 'tensor')), may hold values from -6 to 6
- norm_gain: float32 [4096], replicated, may hold values from 0.25 to 1.75
- expert_ids: int32 [512, 8], P(('groups', 'expert', 'tensor')), may hold values from 0 to 15, all different within a row; in each aligned block of 16 rows (0 to 15, 16 to 31, ...) at most 16 rows name the same one
- route_weight: int32 [512, 8], P(('groups', 'expert', 'tensor')), may hold values from 256 to 4095
- w_gate: bfloat16 [32, 4096, 384], P(('expert', 'tensor')), may hold values from -0.09375 to 0.09375
- w_up: bfloat16 [32, 4096, 384], P(('expert', 'tensor')), may hold values from -0.09375 to 0.09375
- w_down: bfloat16 [32, 384, 4096], P(('expert', 'tensor')), may hold values from -0.21875 to 0.21875
Outputs:
- layer_out: bfloat16 [512, 4096], P(('groups', 'expert', 'tensor'))
The draws below stay inside these ranges and needn't reach their ends.
Inputs may be any that keep to these rules, and one draw needn't show every extreme that they name: `expert_ids`: each row names 8 different experts; among the 16 rows of one device no expert is named by more than 16 rows, a bound that some block reaches.
All inputs are finite; a program needn't handle non-finite values.
Results may differ from the reference program's by a relative error of at most 0.015.
Values may be sent and summed in bfloat16 or wider, within the bound.
A program may use at most 64 MiB of HBM per device.

```python
import math
import jax
import jax.numpy as jnp
import numpy as np
from jax import lax

D = 4096
H = 768
TOPK = 8
TOK_DEV = 16
EXPERTS = 16
CAP = 16
TOKENS = 512
N_TENSOR = 4


def plant(entries, own_key, smallest, high):
    extent = entries.shape
    place = [jax.random.randint(jax.random.fold_in(own_key, axis), (), 0, extent[axis]) for axis in range(len(extent))]
    entries = entries.at[tuple(place)].set(smallest)
    longest = extent.index(max(extent))
    place[longest] = (place[longest] + 1) % extent[longest]
    return entries.at[tuple(place)].set(high)


def raised(array, key, source, target, shards_of, factor):
    owner, partner = [(jnp.arange(array.shape[dim]) // (array.shape[dim] // shards_of)).reshape([-1 if axis == dim else 1 for axis in range(array.ndim)]) for dim in (source, target)]
    chosen = jax.random.permutation(key, shards_of)[partner]
    strong = (owner == chosen) | (owner == (partner + shards_of // 2) % shards_of)
    return jnp.where(strong, factor * array, array)


def levels(stream_key, dims, pieces, smallest, largest):
    gain = 1.0
    for dim, blocks in pieces:
        steps = jax.random.uniform(jax.random.fold_in(jax.random.fold_in(stream_key, 6), dim), (blocks,), jnp.float32, smallest / len(pieces), largest / len(pieces))
        gain = gain * jnp.repeat(jnp.exp(steps), dims[dim] // blocks).reshape((-1,) + (1,) * (len(dims) - 1 - dim))
    return gain


def routed_block(stream_key, own, number, rows, count, top, reach, slope):
    sequence = jax.random.permutation(stream_key, count)
    packed, usual = portions_of(count, rows * top, reach, slope, True), portions_of(count, rows * top, reach, slope, False)
    places = jnp.arange(count)

    def named(sizes, rotation):
        used = int((sizes > 0).sum())
        fixed = max(1, used // 4)
        shifted = fixed + (places - fixed + rotation * (used - fixed)) % max(1, count - fixed)
        return jnp.zeros((count,), jnp.int32).at[sequence[jnp.where(places < fixed, places, shifted)]].set(jnp.asarray(sizes, jnp.int32))

    sizes = jnp.where(number % 4 == 0, named(packed, number // 4), named(usual, number - number // 4 - 1))
    mixed = jax.random.permutation(jax.random.fold_in(own, 3), count)
    donor, receiver = mixed[0:count // 2 * 2:2], mixed[1:count // 2 * 2:2]
    room = jnp.minimum(sizes[donor] - 1, reach - sizes[receiver]) // 2
    room = jnp.where((donor == sequence[0]) | (receiver == sequence[0]) | (sizes[receiver] == 0), 0, jnp.maximum(room, 0))
    shifted = jax.random.randint(jax.random.fold_in(own, 4), (count // 2,), 0, 1 << 20) % (room + 1)
    sizes = sizes.at[donor].add(-shifted).at[receiver].add(shifted)
    labels = jnp.searchsorted(jnp.cumsum(sizes), jnp.arange(rows * top), side="right").astype(jnp.int32)
    listing = labels.reshape(top, rows).T
    listing = listing[jax.random.permutation(jax.random.fold_in(own, 1), rows)]
    rotation = jax.random.randint(jax.random.fold_in(own, 2), (rows, 1), 0, top)
    return jnp.take_along_axis(listing, (jnp.arange(top)[None, :] + rotation) % top, axis=1)


def portions_of(count, total, reach, lean, full):
    portions = [(1 << 20) // math.isqrt(grade ** lean) + 1 for grade in range(1, count + 1)]
    largest = reach if full else min(reach, max(-(-total // count), total * portions[0] // sum(portions)))
    least = 1 if total - largest >= count - 1 else 0
    holding, rest = [largest] + [least] * (count - 1), total - largest - least * (count - 1)
    while rest > 0:
        candidates = [i for i in range(1, count) if holding[i] < largest] or [i for i in range(1, count) if holding[i] < reach]
        pool, budget = sum([portions[i] for i in candidates]), rest
        for i in candidates:
            extra = min(reach - holding[i], max(1, budget * portions[i] // pool), rest)
            holding[i] = holding[i] + extra
            rest = rest - extra
    return np.array(holding)


def noise(stream_key, extent, spread, most, shards=(), held_as=jnp.bfloat16):
    array = jax.random.normal(stream_key, extent, jnp.float32) * spread
    if len(shards) > 0:
        array = levels(stream_key, extent, shards, -0.22, 0.18) * array
    return jnp.clip(array, min=-most, max=most).astype(held_as)


def heavy_noise(key, dims, scale, reach, pieces, heavy, held_as=jnp.bfloat16):
    drawn = scale * jax.random.normal(key, dims, jnp.float32)
    if pieces:
        drawn = drawn * levels(key, dims, pieces, -0.22, 0.18)
    return jnp.clip(raised(drawn, jax.random.fold_in(key, 3), *heavy), -reach, reach).astype(held_as)


def setup_inputs(seed: int = 0, part: int = 0) -> dict:
    splits = jax.random.split(jax.random.key(seed), 9)
    own_keys = jax.random.split(jax.random.fold_in(splits[8], part), 9)
    attn_partial = heavy_noise(own_keys[0], (N_TENSOR, TOKENS, D), 1.0, 6.0, ((0, 4), (1, 8)), (0, 1, 4, 2.0))
    residual = noise(own_keys[1], (TOKENS, D), 1.0, 6.0, ((0, 32),))
    norm_gain = jnp.clip(1.0 + 0.15 * jax.random.normal(splits[2], (D,), jnp.float32), 0.25, 1.75)
    expert_ids_keys = jax.random.split(jax.random.fold_in(own_keys[3], 1), TOKENS // TOK_DEV)
    expert_ids_turns = jax.random.permutation(jax.random.fold_in(own_keys[3], 3), TOKENS // TOK_DEV)
    expert_ids = jax.vmap(lambda own, number: routed_block(jax.random.fold_in(own_keys[3], 2), own, number, TOK_DEV, EXPERTS, TOPK, CAP, 2))(expert_ids_keys, expert_ids_turns).reshape((TOKENS, TOPK))
    route_weight = plant(jax.random.randint(own_keys[4], (TOKENS, TOPK), 256, 4096), jax.random.fold_in(own_keys[4], 1), 256, 4095).astype(jnp.int32)
    w_gate = noise(splits[5], (2 * EXPERTS, D, H // 2), D ** -0.5, 0.09375, ((0, 32),))
    w_up = noise(splits[6], (2 * EXPERTS, D, H // 2), D ** -0.5, 0.09375, ((0, 32),))
    w_down = noise(splits[7], (2 * EXPERTS, H // 2, D), H ** -0.5, 0.21875, ((0, 32),))
    return {"attn_partial": attn_partial, "residual": residual, "norm_gain": norm_gain, "expert_ids": expert_ids, "route_weight": route_weight, "w_gate": w_gate, "w_up": w_up, "w_down": w_down}


epsilon = 1e-06

def reference(attn_partial, residual, norm_gain, expert_ids, route_weight, w_gate, w_up, w_down):
    attn_total = lax.optimization_barrier(jnp.sum(attn_partial.astype(jnp.float32), axis=0))
    stream = residual.astype(jnp.float32) + attn_total
    scale = lax.rsqrt(lax.optimization_barrier(jnp.mean(stream * stream, axis=-1, keepdims=True)) + epsilon)
    normed = (stream * scale * norm_gain).astype(jnp.bfloat16)
    blocks = TOKENS // TOK_DEV
    block_ids = expert_ids.reshape(blocks, TOK_DEV, TOPK)
    block_weights = (route_weight.astype(jnp.float32) / 2048.0).reshape(blocks, TOK_DEV, TOPK)
    block_rows = normed.astype(jnp.float32).reshape(blocks, TOK_DEV, D)
    slots = jnp.arange(CAP, dtype=jnp.int32)

    def one_expert(expert):
        picked = block_ids == expert
        chosen = jnp.any(picked, axis=-1)
        weighting = lax.optimization_barrier(jnp.sum(jnp.where(picked, block_weights, jnp.float32(0.0)), axis=-1))
        position = (jnp.cumsum(chosen.astype(jnp.int32), axis=1) - 1).astype(jnp.int32)
        selector = (chosen[:, None, :] & (position[:, None, :] == slots[None, :, None])).astype(jnp.float32)
        gathered = jnp.einsum('bct,btd->bcd', selector, block_rows, precision=lax.Precision.HIGHEST)
        gathered = gathered.astype(jnp.bfloat16).reshape(blocks * CAP, D)
        summed = jnp.zeros((blocks * CAP, D), jnp.float32)
        for half in range(2):
            slot_index = (2 * expert + half).astype(jnp.int32)
            gate_piece = lax.dynamic_index_in_dim(w_gate, slot_index, 0, keepdims=False)
            up_piece = lax.dynamic_index_in_dim(w_up, slot_index, 0, keepdims=False)
            down_piece = lax.dynamic_index_in_dim(w_down, slot_index, 0, keepdims=False)
            gate_out = jnp.dot(gathered, gate_piece, preferred_element_type=jnp.float32)
            up_out = jnp.dot(gathered, up_piece, preferred_element_type=jnp.float32)
            activated = (jax.nn.silu(gate_out) * up_out).astype(jnp.bfloat16)
            half_out = jnp.dot(activated, down_piece, preferred_element_type=jnp.float32).astype(jnp.bfloat16)
            summed = summed + half_out.astype(jnp.float32)
        combined = summed.reshape(blocks, CAP, D)
        return jnp.einsum('bct,bcd->btd', selector * weighting[:, None, :], combined, precision=lax.Precision.HIGHEST)

    def accumulate(expert, running):
        return running + one_expert(expert)
    expert_mix = lax.fori_loop(0, EXPERTS, accumulate, jnp.zeros((blocks, TOK_DEV, D), jnp.float32))
    return (stream + expert_mix.reshape(TOKENS, D)).astype(jnp.bfloat16)
```

```python
import functools

import jax
import jax.numpy as jnp
from jax import lax
from jax.experimental import pallas as pl
from jax.experimental.pallas import tpu as pltpu
from jax.sharding import PartitionSpec as P

epsilon = 1e-06
MESH = pl.DeviceIdType.MESH
EXTRA = 128


def kernel(
    attn_ref, res_ref, gain_ref, ids_ref, rw_ref, wg_hbm, wu_hbm, wd_hbm,
    out_ref,
    wg, wu, wd, own_attn, attn_in, stream, rows, part, mate_in, s_in, f_in, z_in,
    w_sem, attn_send, attn_recv, zg_send, zg_recv, pg_send, pg_recv, mg_send, mg_recv,
    mr_send, mr_recv, sr_send, sr_recv, fr_send, fr_recv, zr_send, zr_recv,
):
    width = res_ref.shape[1]
    tok = res_ref.shape[0]
    e = lax.axis_index("expert")
    z = lax.axis_index("tensor")
    y, x, c = e // 4, (e // 2) % 2, e % 2
    fx, fy = (x + 1 - c) % 2, (y + c) % 2
    sx, sy = (x + c) % 2, (y + 1 - c) % 2
    p_me, p_f, p_s, p_d = 2 * y + x, 2 * fy + fx, 2 * sy + sx, 2 * (1 - y) + (1 - x)
    mate_core = 1 - c

    def at_z(k):
        return ((z // 2 + k // 2) % 2) * 2 + (z + k) % 2

    first = {"expert": 2 * p_f + c, "tensor": z}
    second = {"expert": 2 * p_s + c, "tensor": z}
    mate = {"expert": 2 * p_me + mate_core, "tensor": z}

    def along(k):
        return {"expert": e, "tensor": at_z(k)}

    sent = []

    def send(src, dst, send_sem, recv_sem, to):
        copy = pltpu.make_async_remote_copy(
            src_ref=src, dst_ref=dst, send_sem=send_sem, recv_sem=recv_sem,
            device_id=to, device_id_type=MESH,
        )
        copy.start()
        sent.append(copy)

    def arrived(dst, send_sem, recv_sem, frm):
        pltpu.make_async_remote_copy(
            src_ref=dst, dst_ref=dst, send_sem=send_sem, recv_sem=recv_sem,
            device_id=frm, device_id_type=MESH,
        ).wait_recv()

    loads = [
        pltpu.make_async_copy(attn_ref.at[z], own_attn, w_sem.at[3]),
        pltpu.make_async_copy(wg_hbm, wg, w_sem.at[0]),
        pltpu.make_async_copy(wu_hbm, wu, w_sem.at[1]),
        pltpu.make_async_copy(wd_hbm, wd, w_sem.at[2]),
    ]
    for load in loads:
        load.start()

    barrier = pltpu.get_barrier_semaphore()
    for other in (first, second, mate, along(1), along(2), along(3)):
        pl.semaphore_signal(barrier, inc=1, device_id=other, device_id_type=MESH)
    pl.semaphore_wait(barrier, 6)

    for k in (1, 2, 3):
        send(attn_ref.at[at_z(k)], attn_in.at[k - 1], attn_send.at[k - 1], attn_recv.at[k - 1], along(k))

    column = lax.broadcasted_iota(jnp.int32, (tok, EXTRA), 1)
    whole = jnp.zeros((tok, EXTRA), jnp.int32)
    for j in range(ids_ref.shape[1]):
        whole = whole + jnp.where(column % 64 == ids_ref[:, j : j + 1], rw_ref[:, j : j + 1], 0)
    low = whole & 15
    pieces = jnp.where(column < 64, whole - low, low)
    rows[z, c, p_me, :, width:] = pieces.astype(jnp.float32).astype(jnp.bfloat16)

    loads[0].wait()
    total = res_ref[...].astype(jnp.float32) + own_attn[...].astype(jnp.float32)
    for k in (1, 2, 3):
        arrived(attn_in.at[k - 1], attn_send.at[k - 1], attn_recv.at[k - 1], along(k))
        total = total + attn_in[k - 1].astype(jnp.float32)
    stream[...] = total
    scale = lax.rsqrt(jnp.mean(total * total, axis=-1, keepdims=True) + epsilon)
    rows[z, c, p_me, :, :width] = (stream[...] * scale * gain_ref[...]).astype(jnp.bfloat16)

    def spread(k):
        q = at_z(k)
        mine = rows.at[q, c, p_me]
        send(mine, mine, pg_send.at[k, 0], pg_recv.at[k, 0], first)
        send(mine, mine, pg_send.at[k, 1], pg_recv.at[k, 1], second)
        send(mine, mine, mg_send.at[k, 0], mg_recv.at[k, 0], mate)

    def z_step(k):
        arrived(rows.at[at_z(k), c, p_me], zg_send.at[k - 1], zg_recv.at[k - 1], along(k))
        spread(k)

    def f_step(k):
        block = rows.at[at_z(k), c, p_f]
        arrived(block, pg_send.at[k, 0], pg_recv.at[k, 0], first)
        send(block, block, pg_send.at[k, 2], pg_recv.at[k, 2], second)
        send(block, block, mg_send.at[k, 1], mg_recv.at[k, 1], mate)

    def s_step(k):
        block = rows.at[at_z(k), c, p_s]
        arrived(block, pg_send.at[k, 1], pg_recv.at[k, 1], second)
        send(block, block, mg_send.at[k, 2], mg_recv.at[k, 2], mate)

    def d_step(k):
        block = rows.at[at_z(k), c, p_d]
        arrived(block, pg_send.at[k, 2], pg_recv.at[k, 2], second)
        send(block, block, mg_send.at[k, 3], mg_recv.at[k, 3], mate)

    expert = (e * lax.axis_size("tensor") + z) // 2

    def compute(k):
        q = at_z(k)
        for j, p in enumerate((p_me, p_s, p_f, p_d)):
            arrived(rows.at[q, mate_core, p], mg_send.at[k, j], mg_recv.at[k, j], mate)
        chunk = 8 * tok
        tail = rows[q, :, :, :, width:].reshape(chunk, EXTRA).astype(jnp.float32)
        col = lax.broadcasted_iota(jnp.int32, (chunk, EXTRA), 1)
        weight = jnp.sum(jnp.where(col % 64 == expert, tail, 0.0), axis=-1, keepdims=True) / 2048.0
        values = rows[q, :, :, :, :width].reshape(chunk, width)
        gate = jnp.dot(values, wg[...], preferred_element_type=jnp.float32)
        up = jnp.dot(values, wu[...], preferred_element_type=jnp.float32)
        act = (gate / (1.0 + jnp.exp(-gate)) * up).astype(jnp.bfloat16)
        step = min(1024, width)
        for n in range(0, width, step):
            half = jnp.dot(act, wd[:, n : n + step], preferred_element_type=jnp.float32)
            part[k, :, :, :, n : n + step] = (half * weight).astype(jnp.bfloat16).reshape(2, 4, tok, step)
        send(part.at[k, mate_core], mate_in.at[k], mr_send.at[k], mr_recv.at[k], mate)

    def add(k, p, arriving):
        part[k, c, p] = (part[k, c, p].astype(jnp.float32) + arriving.astype(jnp.float32)).astype(jnp.bfloat16)

    def back_s(k):
        arrived(mate_in.at[k], mr_send.at[k], mr_recv.at[k], mate)
        for j, p in enumerate((p_s, p_d)):
            add(k, p, mate_in[k, p])
            send(part.at[k, c, p], s_in.at[k, j], sr_send.at[k, j], sr_recv.at[k, j], second)
        for p in (p_f, p_me):
            add(k, p, mate_in[k, p])

    def back_f(k):
        arrived(s_in.at[k, 1], sr_send.at[k, 1], sr_recv.at[k, 1], second)
        add(k, p_f, s_in[k, 1])
        send(part.at[k, c, p_f], f_in.at[k], fr_send.at[k], fr_recv.at[k], first)
        arrived(s_in.at[k, 0], sr_send.at[k, 0], sr_recv.at[k, 0], second)
        add(k, p_me, s_in[k, 0])

    def back_z(k):
        arrived(f_in.at[k], fr_send.at[k], fr_recv.at[k], first)
        if k == 0:
            stream[...] = stream[...] + part[0, c, p_me].astype(jnp.float32) + f_in[0].astype(jnp.float32)
        else:
            add(k, p_me, f_in[k])
            send(part.at[k, c, p_me], z_in.at[k - 1], zr_send.at[k - 1], zr_recv.at[k - 1], along(k))

    spread(0)
    own = rows.at[z, c, p_me]
    for k in (1, 2, 3):
        send(own, own, zg_send.at[k - 1], zg_recv.at[k - 1], along(k))

    f_step(0)
    z_step(1)
    s_step(0)
    d_step(0)
    f_step(1)
    z_step(2)
    s_step(1)
    d_step(1)
    for load in loads[1:]:
        load.wait()
    compute(0)
    f_step(2)
    z_step(3)
    s_step(2)
    d_step(2)
    compute(1)
    back_s(0)
    f_step(3)
    s_step(3)
    d_step(3)
    compute(2)
    back_s(1)
    back_f(0)
    compute(3)
    back_s(2)
    back_f(1)
    back_z(0)
    back_s(3)
    back_f(2)
    back_z(1)
    back_f(3)
    back_z(2)
    back_z(3)

    total = stream[...]
    for k in (1, 2, 3):
        arrived(z_in.at[k - 1], zr_send.at[k - 1], zr_recv.at[k - 1], along(k))
        total = total + z_in[k - 1].astype(jnp.float32)
    out_ref[...] = total.astype(out_ref.dtype)
    for copy in sent:
        copy.wait_send()


def gather_body(attn_partial, residual, norm_gain, expert_ids, route_weight, w_gate, w_up, w_down):
    tok, width = residual.shape
    hidden = w_gate.shape[2]
    bf16 = jnp.bfloat16
    dma = pltpu.SemaphoreType.DMA
    vmem = pl.BlockSpec(memory_space=pltpu.VMEM)
    hbm = pl.BlockSpec(memory_space=pl.ANY)
    return pl.pallas_call(
        kernel,
        out_shape=jax.ShapeDtypeStruct((tok, width), bf16),
        in_specs=[hbm, vmem, vmem, vmem, vmem, hbm, hbm, hbm],
        out_specs=vmem,
        scratch_shapes=[
            pltpu.VMEM((width, hidden), bf16),
            pltpu.VMEM((width, hidden), bf16),
            pltpu.VMEM((hidden, width), bf16),
            pltpu.VMEM((tok, width), bf16),
            pltpu.VMEM((3, tok, width), bf16),
            pltpu.VMEM((tok, width), jnp.float32),
            pltpu.VMEM((4, 2, 4, tok, width + EXTRA), bf16),
            pltpu.VMEM((4, 2, 4, tok, width), bf16),
            pltpu.VMEM((4, 4, tok, width), bf16),
            pltpu.VMEM((4, 2, tok, width), bf16),
            pltpu.VMEM((4, tok, width), bf16),
            pltpu.VMEM((3, tok, width), bf16),
            dma((4,)),
            dma((3,)), dma((3,)),
            dma((3,)), dma((3,)),
            dma((4, 3)), dma((4, 3)),
            dma((4, 4)), dma((4, 4)),
            dma((4,)), dma((4,)),
            dma((4, 2)), dma((4, 2)),
            dma((4,)), dma((4,)),
            dma((3,)), dma((3,)),
        ],
        compiler_params=pltpu.CompilerParams(
            collective_id=0, has_side_effects=True, vmem_limit_bytes=48 * 1024 * 1024
        ),
        cost_estimate=pl.CostEstimate(
            flops=6 * 32 * tok * width * hidden,
            bytes_accessed=6 * width * hidden,
            transcendentals=32 * tok * hidden,
        ),
    )(
        attn_partial.reshape(-1, tok, width), residual, norm_gain.reshape(1, width),
        expert_ids, route_weight, w_gate[0], w_up[0], w_down[0],
    )


def slots_body(attn_partial, residual, norm_gain, expert_ids, route_weight, w_gate, w_up, w_down):
    width = residual.shape[1]
    tok_rows = residual.shape[0]
    top_picks = expert_ids.shape[1]
    n_expert = lax.axis_size("expert")
    n_tensor = lax.axis_size("tensor")
    experts = n_expert * n_tensor // 2
    capacity = max(2, min(tok_rows, 2 * tok_rows * top_picks // experts))
    attn_total = lax.psum_scatter(
        attn_partial[0].astype(jnp.float32).astype(jnp.bfloat16),
        "tensor",
        scatter_dimension=0,
        tiled=True,
    ).astype(jnp.float32)
    stream = residual.astype(jnp.float32) + attn_total
    scale = lax.rsqrt(jnp.mean(stream * stream, axis=-1, keepdims=True) + epsilon)
    normed = (stream * scale * norm_gain).astype(jnp.bfloat16)
    weights = route_weight.astype(jnp.float32) / 2048.0
    picked = expert_ids[None, :, :] == jnp.arange(experts, dtype=jnp.int32)[:, None, None]
    chosen = jnp.any(picked, axis=-1)
    weighting = jnp.sum(jnp.where(picked, weights[None, :, :], jnp.float32(0.0)), axis=-1)
    position = jnp.cumsum(chosen.astype(jnp.int32), axis=1) - 1
    slots = jnp.arange(capacity, dtype=jnp.int32)
    selector = chosen[:, None, :] & (position[:, None, :] == slots[None, :, None])
    gathered = jnp.einsum(
        "ect,td->ecd", selector.astype(jnp.bfloat16), normed, preferred_element_type=jnp.float32
    ).astype(jnp.bfloat16)
    outgoing = jnp.broadcast_to(gathered[:, None], (experts, 2, capacity, width))
    direct_send = outgoing.reshape(n_expert * n_tensor, capacity, width)
    incoming = lax.all_to_all(
        direct_send, ("expert", "tensor"), split_axis=0, concat_axis=0, tiled=True
    )
    flattened = incoming.reshape(-1, width)
    gate_out = jnp.dot(flattened, w_gate[0], preferred_element_type=jnp.float32)
    up_out = jnp.dot(flattened, w_up[0], preferred_element_type=jnp.float32)
    activated = (jax.nn.silu(gate_out) * up_out).astype(jnp.bfloat16)
    half_out = jnp.dot(activated, w_down[0], preferred_element_type=jnp.float32).astype(
        jnp.bfloat16
    )
    returned = lax.all_to_all(
        half_out.reshape(incoming.shape),
        ("expert", "tensor"),
        split_axis=0,
        concat_axis=0,
        tiled=True,
    )
    returned = returned.reshape(experts, 2, capacity, width)
    combined = returned[:, 0].astype(jnp.float32) + returned[:, 1].astype(jnp.float32)
    mixing = selector.astype(jnp.float32) * weighting[:, None, :]
    expert_mix = jnp.einsum("ect,ecd->td", mixing, combined, precision=lax.Precision.HIGHEST)
    return (stream + expert_mix).astype(jnp.bfloat16)


def solution(mesh):
    in_specs = (
        P("tensor", ("groups", "expert"), None),
        P(("groups", "expert", "tensor"), None),
        P(),
        P(("groups", "expert", "tensor"), None),
        P(("groups", "expert", "tensor"), None),
        P(("expert", "tensor"), None, None),
        P(("expert", "tensor"), None, None),
        P(("expert", "tensor"), None, None),
    )
    out_specs = P(("groups", "expert", "tensor"), None)
    dense = (mesh.shape["expert"], mesh.shape["tensor"]) == (8, 4)
    body = gather_body if dense else slots_body
    return jax.shard_map(body, mesh=mesh, in_specs=in_specs, out_specs=out_specs, check_vma=False)
```

```python
import functools

import jax
import jax.numpy as jnp
from jax import lax
from jax.experimental import pallas as pl
from jax.experimental.pallas import tpu as pltpu
from jax.sharding import PartitionSpec as P

epsilon = 1e-06
MESH = pl.DeviceIdType.MESH
EXTRA = 128


def kernel(
    attn_ref, res_hbm, gain_hbm, ids_hbm, rw_hbm, wg_hbm, wu_hbm, wd_hbm,
    out_ref,
    res_ref, gain_ref, ids_ref, rw_ref, wg, wu, wd, own_attn, attn_in, stream, rows, part, mate_in, s_in, f_in, z_in,
    w_sem, attn_send, attn_recv, zg_send, zg_recv, pg_send, pg_recv, mg_send, mg_recv,
    mr_send, mr_recv, sr_send, sr_recv, fr_send, fr_recv, zr_send, zr_recv,
):
    width = res_ref.shape[1]
    tok = res_ref.shape[0]
    e = lax.axis_index("expert")
    z = lax.axis_index("tensor")
    y, x, c = e // 4, (e // 2) % 2, e % 2
    fx, fy = (x + 1 - c) % 2, (y + c) % 2
    sx, sy = (x + c) % 2, (y + 1 - c) % 2
    p_me, p_f, p_s, p_d = 2 * y + x, 2 * fy + fx, 2 * sy + sx, 2 * (1 - y) + (1 - x)
    mate_core = 1 - c

    flip = z // 2
    inner = z + flip * (3 - 2 * z)

    def at_z(k):
        near = k + inner * ((k == 0) - (k == 1))
        return near + flip * (3 - 2 * near)

    def side(k):
        return (1 - 2 * inner * (k == 1)) * (1 - 2 * flip)

    first = {"expert": 2 * p_f + c, "tensor": z}
    second = {"expert": 2 * p_s + c, "tensor": z}
    mate = {"expert": 2 * p_me + mate_core, "tensor": z}

    def column(other):
        return {"expert": e, "tensor": other}

    sent = []

    def send(src, dst, send_sem, recv_sem, to):
        copy = pltpu.make_async_remote_copy(
            src_ref=src, dst_ref=dst, send_sem=send_sem, recv_sem=recv_sem,
            device_id=to, device_id_type=MESH,
        )
        copy.start()
        sent.append(copy)

    def arrived(dst, send_sem, recv_sem, frm):
        pltpu.make_async_remote_copy(
            src_ref=dst, dst_ref=dst, send_sem=send_sem, recv_sem=recv_sem,
            device_id=frm, device_id_type=MESH,
        ).wait_recv()

    loads = [
        pltpu.make_async_copy(ids_hbm, ids_ref, w_sem.at[3]),
        pltpu.make_async_copy(rw_hbm, rw_ref, w_sem.at[4]),
        pltpu.make_async_copy(attn_ref.at[z], own_attn, w_sem.at[5]),
        pltpu.make_async_copy(res_hbm, res_ref, w_sem.at[6]),
        pltpu.make_async_copy(gain_hbm, gain_ref, w_sem.at[7]),
        pltpu.make_async_copy(wg_hbm, wg, w_sem.at[0]),
        pltpu.make_async_copy(wu_hbm, wu, w_sem.at[1]),
        pltpu.make_async_copy(wd_hbm, wd, w_sem.at[2]),
    ]
    for load in loads:
        load.start()

    barrier = pltpu.get_barrier_semaphore()
    for other in (first, second, mate) + tuple(column((z + k) % 4) for k in (1, 2, 3)):
        pl.semaphore_signal(barrier, inc=1, device_id=other, device_id_type=MESH)
    pl.semaphore_wait(barrier, 6)

    for k in (1, 2, 3):
        other = (z + k) % 4
        send(attn_ref.at[other], attn_in.at[k - 1], attn_send.at[k - 1], attn_recv.at[k - 1], column(other))

    for load in loads[:2]:
        load.wait()
    place = lax.broadcasted_iota(jnp.int32, (EXTRA, tok), 0)
    whole = jnp.zeros((EXTRA, tok), jnp.int32)
    for j in range(ids_ref.shape[0]):
        whole = whole + jnp.where(place % 64 == ids_ref[j : j + 1, :], rw_ref[j : j + 1, :], 0)
    low = whole & 15
    pieces = jnp.where(place < 64, whole - low, low).astype(jnp.float32).astype(jnp.bfloat16)
    line = lax.broadcasted_iota(jnp.int32, (tok, tok), 0)
    across = lax.broadcasted_iota(jnp.int32, (tok, tok), 1)
    same = (line == across).astype(jnp.float32).astype(jnp.bfloat16)
    turned = lax.dot_general(same, pieces, (((1,), (1,)), ((), ())), preferred_element_type=jnp.float32)
    rows[z, c, p_me, :, width:] = turned.astype(jnp.bfloat16)

    for load in loads[2:5]:
        load.wait()
    total = res_ref[...].astype(jnp.float32) + own_attn[...].astype(jnp.float32)
    for k in (1, 2, 3):
        arrived(attn_in.at[k - 1], attn_send.at[k - 1], attn_recv.at[k - 1], column((z + 4 - k) % 4))
        total = total + attn_in[k - 1].astype(jnp.float32)
    stream[...] = total
    scale = lax.rsqrt(jnp.mean(total * total, axis=-1, keepdims=True) + epsilon)
    rows[z, c, p_me, :, :width] = (stream[...] * scale * gain_ref[...]).astype(jnp.bfloat16)

    def hop(slot, q, to):
        block = rows.at[q, c, p_me]
        return pltpu.make_async_remote_copy(
            src_ref=block, dst_ref=block, send_sem=zg_send.at[slot], recv_sem=zg_recv.at[q],
            device_id=column(to), device_id_type=MESH,
        )

    def spread(k):
        q = at_z(k)
        mine = rows.at[q, c, p_me]
        send(mine, mine, pg_send.at[k, 0], pg_recv.at[k, 0], first)
        send(mine, mine, pg_send.at[k, 1], pg_recv.at[k, 1], second)
        send(mine, mine, mg_send.at[k, 0], mg_recv.at[k, 0], mate)

    def z_step(k):
        q = at_z(k)
        block = rows.at[q, c, p_me]
        arrived(block, zg_send.at[k], zg_recv.at[q], column(z + side(k)))

        @pl.when(inner == 1)
        def _():
            hop(k, q, z - side(k)).start()

        spread(k)

    def f_step(k):
        block = rows.at[at_z(k), c, p_f]
        arrived(block, pg_send.at[k, 0], pg_recv.at[k, 0], first)
        send(block, block, pg_send.at[k, 2], pg_recv.at[k, 2], second)
        send(block, block, mg_send.at[k, 1], mg_recv.at[k, 1], mate)

    def s_step(k):
        block = rows.at[at_z(k), c, p_s]
        arrived(block, pg_send.at[k, 1], pg_recv.at[k, 1], second)
        send(block, block, mg_send.at[k, 2], mg_recv.at[k, 2], mate)

    def d_step(k):
        block = rows.at[at_z(k), c, p_d]
        arrived(block, pg_send.at[k, 2], pg_recv.at[k, 2], second)
        send(block, block, mg_send.at[k, 3], mg_recv.at[k, 3], mate)

    expert = (e * lax.axis_size("tensor") + z) // 2

    def compute(k):
        q = at_z(k)
        for j, p in enumerate((p_me, p_s, p_f, p_d)):
            arrived(rows.at[q, mate_core, p], mg_send.at[k, j], mg_recv.at[k, j], mate)
        chunk = 8 * tok
        tail = rows[q, :, :, :, width:].reshape(chunk, EXTRA).astype(jnp.float32)
        col = lax.broadcasted_iota(jnp.int32, (chunk, EXTRA), 1)
        weight = jnp.sum(jnp.where(col % 64 == expert, tail, 0.0), axis=-1, keepdims=True) / 2048.0
        values = rows[q, :, :, :, :width].reshape(chunk, width)
        gate = jnp.dot(values, wg[...], preferred_element_type=jnp.float32)
        up = jnp.dot(values, wu[...], preferred_element_type=jnp.float32)
        act = (gate / (1.0 + jnp.exp(-gate)) * up).astype(jnp.bfloat16)
        step = min(1024, width)
        for n in range(0, width, step):
            half = jnp.dot(act, wd[:, n : n + step], preferred_element_type=jnp.float32)
            part[k, :, :, :, n : n + step] = (half * weight).astype(jnp.bfloat16).reshape(2, 4, tok, step)
        send(part.at[k, mate_core], mate_in.at[k], mr_send.at[k], mr_recv.at[k], mate)

    def add(k, p, arriving):
        part[k, c, p] = (part[k, c, p].astype(jnp.float32) + arriving.astype(jnp.float32)).astype(jnp.bfloat16)

    def back_s(k):
        arrived(mate_in.at[k], mr_send.at[k], mr_recv.at[k], mate)
        for j, p in enumerate((p_s, p_d)):
            add(k, p, mate_in[k, p])
            send(part.at[k, c, p], s_in.at[k, j], sr_send.at[k, j], sr_recv.at[k, j], second)
        for p in (p_f, p_me):
            add(k, p, mate_in[k, p])

    def back_f(k):
        arrived(s_in.at[k, 1], sr_send.at[k, 1], sr_recv.at[k, 1], second)
        add(k, p_f, s_in[k, 1])
        send(part.at[k, c, p_f], f_in.at[k], fr_send.at[k], fr_recv.at[k], first)
        arrived(s_in.at[k, 0], sr_send.at[k, 0], sr_recv.at[k, 0], second)
        add(k, p_me, s_in[k, 0])

    def back_z(k):
        arrived(f_in.at[k], fr_send.at[k], fr_recv.at[k], first)
        if k == 0:
            stream[...] = stream[...] + part[0, c, p_me].astype(jnp.float32) + f_in[0].astype(jnp.float32)
        else:
            add(k, p_me, f_in[k])
            send(part.at[k, c, p_me], z_in.at[z], zr_send.at[k - 1], zr_recv.at[z], column(at_z(k)))

    @pl.when(z < 3)
    def _():
        hop(0, z, z + 1).start()

    @pl.when(z > 0)
    def _():
        hop(4, z, z - 1).start()

    spread(0)

    f_step(0)
    z_step(1)
    s_step(0)
    d_step(0)
    z_step(2)
    f_step(1)
    s_step(1)
    z_step(3)
    d_step(1)
    f_step(2)
    for load in loads[5:]: load.wait()
    compute(0)
    s_step(2)
    d_step(2)
    f_step(3)
    compute(1)
    s_step(3)
    d_step(3)
    back_s(1)
    compute(2)
    back_s(2)
    back_f(1)
    compute(3)
    back_s(3)
    back_f(2)
    back_z(1)
    back_s(0)
    back_f(3)
    back_z(2)
    back_f(0)
    back_z(3)
    back_z(0)

    total = stream[...]
    for k in (1, 2, 3):
        q = at_z(k)
        arrived(z_in.at[q], zr_send.at[k - 1], zr_recv.at[q], column(q))
        total = total + z_in[q].astype(jnp.float32)
    out_ref[...] = total.astype(out_ref.dtype)
    for copy in sent:
        copy.wait_send()

    @pl.when(z < 3)
    def _():
        hop(0, z, z + 1).wait_send()

    @pl.when(z > 0)
    def _():
        hop(4, z, z - 1).wait_send()

    @pl.when(inner == 1)
    def _():
        for k in (1, 2, 3):
            hop(k, at_z(k), z - side(k)).wait_send()


def gather_body(attn_partial, residual, norm_gain, expert_ids, route_weight, w_gate, w_up, w_down):
    tok, width = residual.shape
    hidden = w_gate.shape[2]
    bf16 = jnp.bfloat16
    dma = pltpu.SemaphoreType.DMA
    vmem = pl.BlockSpec(memory_space=pltpu.VMEM)
    hbm = pl.BlockSpec(memory_space=pl.ANY)
    return pl.pallas_call(
        kernel,
        out_shape=jax.ShapeDtypeStruct((tok, width), bf16),
        in_specs=[hbm] * 8,
        out_specs=vmem,
        scratch_shapes=[
            pltpu.VMEM((tok, width), bf16),
            pltpu.VMEM((1, width), jnp.float32),
            pltpu.VMEM(expert_ids.shape[::-1], jnp.int32),
            pltpu.VMEM(expert_ids.shape[::-1], jnp.int32),
            pltpu.VMEM((width, hidden), bf16),
            pltpu.VMEM((width, hidden), bf16),
            pltpu.VMEM((hidden, width), bf16),
            pltpu.VMEM((tok, width), bf16),
            pltpu.VMEM((3, tok, width), bf16),
            pltpu.VMEM((tok, width), jnp.float32),
            pltpu.VMEM((4, 2, 4, tok, width + EXTRA), bf16),
            pltpu.VMEM((4, 2, 4, tok, width), bf16),
            pltpu.VMEM((4, 4, tok, width), bf16),
            pltpu.VMEM((4, 2, tok, width), bf16),
            pltpu.VMEM((4, tok, width), bf16),
            pltpu.VMEM((4, tok, width), bf16),
            dma((8,)),
            dma((3,)), dma((3,)),
            dma((5,)), dma((4,)),
            dma((4, 3)), dma((4, 3)),
            dma((4, 4)), dma((4, 4)),
            dma((4,)), dma((4,)),
            dma((4, 2)), dma((4, 2)),
            dma((4,)), dma((4,)),
            dma((3,)), dma((4,)),
        ],
        compiler_params=pltpu.CompilerParams(
            collective_id=0, has_side_effects=True, vmem_limit_bytes=60 * 1024 * 1024
        ),
        cost_estimate=pl.CostEstimate(
            flops=6 * 32 * tok * width * hidden,
            bytes_accessed=6 * width * hidden,
            transcendentals=32 * tok * hidden,
        ),
    )(
        attn_partial.reshape(-1, tok, width), residual, norm_gain.reshape(1, width),
        expert_ids.T, route_weight.T, w_gate[0], w_up[0], w_down[0],
    )


def slots_body(attn_partial, residual, norm_gain, expert_ids, route_weight, w_gate, w_up, w_down):
    width = residual.shape[1]
    tok_rows = residual.shape[0]
    top_picks = expert_ids.shape[1]
    n_expert = lax.axis_size("expert")
    n_tensor = lax.axis_size("tensor")
    experts = n_expert * n_tensor // 2
    capacity = max(2, min(tok_rows, 2 * tok_rows * top_picks // experts))
    attn_total = lax.psum_scatter(
        attn_partial[0].astype(jnp.float32).astype(jnp.bfloat16),
        "tensor",
        scatter_dimension=0,
        tiled=True,
    ).astype(jnp.float32)
    stream = residual.astype(jnp.float32) + attn_total
    scale = lax.rsqrt(jnp.mean(stream * stream, axis=-1, keepdims=True) + epsilon)
    normed = (stream * scale * norm_gain).astype(jnp.bfloat16)
    weights = route_weight.astype(jnp.float32) / 2048.0
    picked = expert_ids[None, :, :] == jnp.arange(experts, dtype=jnp.int32)[:, None, None]
    chosen = jnp.any(picked, axis=-1)
    weighting = jnp.sum(jnp.where(picked, weights[None, :, :], jnp.float32(0.0)), axis=-1)
    position = jnp.cumsum(chosen.astype(jnp.int32), axis=1) - 1
    slots = jnp.arange(capacity, dtype=jnp.int32)
    selector = chosen[:, None, :] & (position[:, None, :] == slots[None, :, None])
    gathered = jnp.einsum(
        "ect,td->ecd", selector.astype(jnp.bfloat16), normed, preferred_element_type=jnp.float32
    ).astype(jnp.bfloat16)
    outgoing = jnp.broadcast_to(gathered[:, None], (experts, 2, capacity, width))
    direct_send = outgoing.reshape(n_expert * n_tensor, capacity, width)
    incoming = lax.all_to_all(
        direct_send, ("expert", "tensor"), split_axis=0, concat_axis=0, tiled=True
    )
    flattened = incoming.reshape(-1, width)
    gate_out = jnp.dot(flattened, w_gate[0], preferred_element_type=jnp.float32)
    up_out = jnp.dot(flattened, w_up[0], preferred_element_type=jnp.float32)
    activated = (jax.nn.silu(gate_out) * up_out).astype(jnp.bfloat16)
    half_out = jnp.dot(activated, w_down[0], preferred_element_type=jnp.float32).astype(
        jnp.bfloat16
    )
    returned = lax.all_to_all(
        half_out.reshape(incoming.shape),
        ("expert", "tensor"),
        split_axis=0,
        concat_axis=0,
        tiled=True,
    )
    returned = returned.reshape(experts, 2, capacity, width)
    combined = returned[:, 0].astype(jnp.float32) + returned[:, 1].astype(jnp.float32)
    mixing = selector.astype(jnp.float32) * weighting[:, None, :]
    expert_mix = jnp.einsum("ect,ecd->td", mixing, combined, precision=lax.Precision.HIGHEST)
    return (stream + expert_mix).astype(jnp.bfloat16)


def solution(mesh):
    in_specs = (
        P("tensor", ("groups", "expert"), None),
        P(("groups", "expert", "tensor"), None),
        P(),
        P(("groups", "expert", "tensor"), None),
        P(("groups", "expert", "tensor"), None),
        P(("expert", "tensor"), None, None),
        P(("expert", "tensor"), None, None),
        P(("expert", "tensor"), None, None),
    )
    out_specs = P(("groups", "expert", "tensor"), None)
    dense = (mesh.shape["expert"], mesh.shape["tensor"]) == (8, 4)
    body = gather_body if dense else slots_body
    return jax.shard_map(body, mesh=mesh, in_specs=in_specs, out_specs=out_specs, check_vma=False)
```

```python
import functools

import jax
import jax.numpy as jnp
from jax import lax
from jax.experimental import pallas as pl
from jax.experimental.pallas import tpu as pltpu
from jax.sharding import PartitionSpec as P

epsilon = 1e-06
MESH = pl.DeviceIdType.MESH
EXTRA = 128


def kernel(
    attn_ref, res_hbm, gain_hbm, ids_hbm, rw_hbm, wg_hbm, wu_hbm, wd_hbm,
    out_ref,
    res_ref, gain_ref, ids_ref, rw_ref, wg, wu, wd, own_attn, attn_in, stream, rows, part, mate_in, s_in, f_in, z_in,
    w_sem, attn_send, attn_recv, zg_send, zg_recv, pg_send, pg_recv, mg_send, mg_recv,
    mr_send, mr_recv, sr_send, sr_recv, fr_send, fr_recv, zr_send, zr_recv,
):
    width = res_ref.shape[1]
    tok = res_ref.shape[0]
    e = lax.axis_index("expert")
    z = lax.axis_index("tensor")
    y, x, c = e // 4, (e // 2) % 2, e % 2
    fx, fy = (x + 1 - c) % 2, (y + c) % 2
    sx, sy = (x + c) % 2, (y + 1 - c) % 2
    p_me, p_f, p_s, p_d = 2 * y + x, 2 * fy + fx, 2 * sy + sx, 2 * (1 - y) + (1 - x)
    mate_core = 1 - c

    flip = z // 2
    inner = z + flip * (3 - 2 * z)

    def at_z(k):
        near = k + inner * ((k == 0) - (k == 1))
        return near + flip * (3 - 2 * near)

    def side(k):
        return (1 - 2 * inner * (k == 1)) * (1 - 2 * flip)

    first = {"expert": 2 * p_f + c, "tensor": z}
    second = {"expert": 2 * p_s + c, "tensor": z}
    mate = {"expert": 2 * p_me + mate_core, "tensor": z}

    def column(other):
        return {"expert": e, "tensor": other}

    sent = []

    def send(src, dst, send_sem, recv_sem, to):
        copy = pltpu.make_async_remote_copy(
            src_ref=src, dst_ref=dst, send_sem=send_sem, recv_sem=recv_sem,
            device_id=to, device_id_type=MESH,
        )
        copy.start()
        sent.append(copy)

    def arrived(dst, send_sem, recv_sem, frm):
        pltpu.make_async_remote_copy(
            src_ref=dst, dst_ref=dst, send_sem=send_sem, recv_sem=recv_sem,
            device_id=frm, device_id_type=MESH,
        ).wait_recv()

    loads = [
        pltpu.make_async_copy(ids_hbm, ids_ref, w_sem.at[3]),
        pltpu.make_async_copy(rw_hbm, rw_ref, w_sem.at[4]),
        pltpu.make_async_copy(attn_ref.at[z], own_attn, w_sem.at[5]),
        pltpu.make_async_copy(res_hbm, res_ref, w_sem.at[6]),
        pltpu.make_async_copy(gain_hbm, gain_ref, w_sem.at[7]),
        pltpu.make_async_copy(wg_hbm, wg, w_sem.at[0]),
        pltpu.make_async_copy(wu_hbm, wu, w_sem.at[1]),
        pltpu.make_async_copy(wd_hbm, wd, w_sem.at[2]),
    ]
    for load in loads:
        load.start()

    barrier = pltpu.get_barrier_semaphore()
    for other in (first, second, mate) + tuple(column((z + k) % 4) for k in (1, 2, 3)):
        pl.semaphore_signal(barrier, inc=1, device_id=other, device_id_type=MESH)
    pl.semaphore_wait(barrier, 6)

    for k in (2, 3, 1):
        other = (z + k) % 4
        send(attn_ref.at[other], attn_in.at[k - 1], attn_send.at[k - 1], attn_recv.at[k - 1], column(other))

    for load in loads[:2]:
        load.wait()
    place = lax.broadcasted_iota(jnp.int32, (EXTRA, tok), 0)
    whole = jnp.zeros((EXTRA, tok), jnp.int32)
    for j in range(ids_ref.shape[0]):
        whole = whole + jnp.where(place % 64 == ids_ref[j : j + 1, :], rw_ref[j : j + 1, :], 0)
    low = whole & 15
    pieces = jnp.where(place < 64, whole - low, low).astype(jnp.float32).astype(jnp.bfloat16)
    line = lax.broadcasted_iota(jnp.int32, (tok, tok), 0)
    across = lax.broadcasted_iota(jnp.int32, (tok, tok), 1)
    same = (line == across).astype(jnp.float32).astype(jnp.bfloat16)
    turned = lax.dot_general(same, pieces, (((1,), (1,)), ((), ())), preferred_element_type=jnp.float32)
    rows[z, c, p_me, :, width:] = turned.astype(jnp.bfloat16)

    for load in loads[2:5]:
        load.wait()
    total = res_ref[...].astype(jnp.float32) + own_attn[...].astype(jnp.float32)
    for k in (1, 2, 3):
        arrived(attn_in.at[k - 1], attn_send.at[k - 1], attn_recv.at[k - 1], column((z + 4 - k) % 4))
        total = total + attn_in[k - 1].astype(jnp.float32)
    stream[...] = total
    scale = lax.rsqrt(jnp.mean(total * total, axis=-1, keepdims=True) + epsilon)
    rows[z, c, p_me, :, :width] = (stream[...] * scale * gain_ref[...]).astype(jnp.bfloat16)

    def hop(slot, q, to):
        block = rows.at[q, c, p_me]
        return pltpu.make_async_remote_copy(
            src_ref=block, dst_ref=block, send_sem=zg_send.at[slot], recv_sem=zg_recv.at[q],
            device_id=column(to), device_id_type=MESH,
        )

    def spread(k):
        q = at_z(k)
        mine = rows.at[q, c, p_me]
        send(mine, mine, pg_send.at[k, 0], pg_recv.at[k, 0], first)
        send(mine, mine, pg_send.at[k, 1], pg_recv.at[k, 1], second)
        send(mine, mine, mg_send.at[k, 0], mg_recv.at[k, 0], mate)

    def z_step(k):
        q = at_z(k)
        block = rows.at[q, c, p_me]
        arrived(block, zg_send.at[k], zg_recv.at[q], column(z + side(k)))

        @pl.when(inner == 1)
        def _():
            hop(k, q, z - side(k)).start()

        spread(k)

    def f_step(k):
        block = rows.at[at_z(k), c, p_f]
        arrived(block, pg_send.at[k, 0], pg_recv.at[k, 0], first)
        send(block, block, pg_send.at[k, 2], pg_recv.at[k, 2], second)
        send(block, block, mg_send.at[k, 1], mg_recv.at[k, 1], mate)

    def s_step(k):
        block = rows.at[at_z(k), c, p_s]
        arrived(block, pg_send.at[k, 1], pg_recv.at[k, 1], second)
        send(block, block, mg_send.at[k, 2], mg_recv.at[k, 2], mate)

    def d_step(k):
        block = rows.at[at_z(k), c, p_d]
        arrived(block, pg_send.at[k, 2], pg_recv.at[k, 2], second)
        send(block, block, mg_send.at[k, 3], mg_recv.at[k, 3], mate)

    expert = (e * lax.axis_size("tensor") + z) // 2

    def compute(k):
        q = at_z(k)
        for j, p in enumerate((p_me, p_s, p_f, p_d)):
            arrived(rows.at[q, mate_core, p], mg_send.at[k, j], mg_recv.at[k, j], mate)
        chunk = 8 * tok
        tail = rows[q, :, :, :, width:].reshape(chunk, EXTRA).astype(jnp.float32)
        col = lax.broadcasted_iota(jnp.int32, (chunk, EXTRA), 1)
        weight = jnp.sum(jnp.where(col % 64 == expert, tail, 0.0), axis=-1, keepdims=True) / 2048.0
        values = rows[q, :, :, :, :width].reshape(chunk, width)
        gate = jnp.dot(values, wg[...], preferred_element_type=jnp.float32)
        up = jnp.dot(values, wu[...], preferred_element_type=jnp.float32)
        act = (gate / (1.0 + jnp.exp(-gate)) * up).astype(jnp.bfloat16)
        step = min(1024, width)
        for n in range(0, width, step):
            half = jnp.dot(act, wd[:, n : n + step], preferred_element_type=jnp.float32)
            part[k, :, :, :, n : n + step] = (half * weight).astype(jnp.bfloat16).reshape(2, 4, tok, step)
        send(part.at[k, mate_core], mate_in.at[k], mr_send.at[k], mr_recv.at[k], mate)

    def add(k, p, arriving):
        part[k, c, p] = (part[k, c, p].astype(jnp.float32) + arriving.astype(jnp.float32)).astype(jnp.bfloat16)

    def back_s(k):
        arrived(mate_in.at[k], mr_send.at[k], mr_recv.at[k], mate)
        for j, p in enumerate((p_s, p_d)):
            add(k, p, mate_in[k, p])
            send(part.at[k, c, p], s_in.at[k, j], sr_send.at[k, j], sr_recv.at[k, j], second)
        for p in (p_f, p_me):
            add(k, p, mate_in[k, p])

    def back_f(k):
        arrived(s_in.at[k, 1], sr_send.at[k, 1], sr_recv.at[k, 1], second)
        add(k, p_f, s_in[k, 1])
        send(part.at[k, c, p_f], f_in.at[k], fr_send.at[k], fr_recv.at[k], first)
        arrived(s_in.at[k, 0], sr_send.at[k, 0], sr_recv.at[k, 0], second)
        add(k, p_me, s_in[k, 0])

    def back_z(k):
        arrived(f_in.at[k], fr_send.at[k], fr_recv.at[k], first)
        if k == 0:
            stream[...] = stream[...] + part[0, c, p_me].astype(jnp.float32) + f_in[0].astype(jnp.float32)
        else:
            add(k, p_me, f_in[k])
            send(part.at[k, c, p_me], z_in.at[z], zr_send.at[k - 1], zr_recv.at[z], column(at_z(k)))

    @pl.when(z < 3)
    def _():
        hop(0, z, z + 1).start()

    @pl.when(z > 0)
    def _():
        hop(4, z, z - 1).start()

    spread(0)

    f_step(0)
    z_step(1)
    s_step(0)
    z_step(2)
    d_step(0)
    f_step(1)
    z_step(3)
    s_step(1)
    d_step(1)
    f_step(2)
    for load in loads[5:]: load.wait()
    compute(0)
    s_step(2)
    f_step(3)
    d_step(2)
    compute(1)
    back_s(1)
    s_step(3)
    d_step(3)
    compute(2)
    back_f(1)
    back_s(2)
    compute(3)
    back_z(1)
    back_s(3)
    back_f(2)
    back_s(0)
    back_z(2)
    back_f(3)
    back_f(0)
    back_z(3)
    back_z(0)

    total = stream[...]
    for k in (1, 2, 3):
        q = at_z(k)
        arrived(z_in.at[q], zr_send.at[k - 1], zr_recv.at[q], column(q))
        total = total + z_in[q].astype(jnp.float32)
    out_ref[...] = total.astype(out_ref.dtype)
    for copy in sent:
        copy.wait_send()

    @pl.when(z < 3)
    def _():
        hop(0, z, z + 1).wait_send()

    @pl.when(z > 0)
    def _():
        hop(4, z, z - 1).wait_send()

    @pl.when(inner == 1)
    def _():
        for k in (1, 2, 3):
            hop(k, at_z(k), z - side(k)).wait_send()


def gather_body(attn_partial, residual, norm_gain, expert_ids, route_weight, w_gate, w_up, w_down):
    tok, width = residual.shape
    hidden = w_gate.shape[2]
    bf16 = jnp.bfloat16
    dma = pltpu.SemaphoreType.DMA
    vmem = pl.BlockSpec(memory_space=pltpu.VMEM)
    hbm = pl.BlockSpec(memory_space=pl.ANY)
    return pl.pallas_call(
        kernel,
        out_shape=jax.ShapeDtypeStruct((tok, width), bf16),
        in_specs=[hbm] * 8,
        out_specs=vmem,
        scratch_shapes=[
            pltpu.VMEM((tok, width), bf16),
            pltpu.VMEM((1, width), jnp.float32),
            pltpu.VMEM(expert_ids.shape[::-1], jnp.int32),
            pltpu.VMEM(expert_ids.shape[::-1], jnp.int32),
            pltpu.VMEM((width, hidden), bf16),
            pltpu.VMEM((width, hidden), bf16),
            pltpu.VMEM((hidden, width), bf16),
            pltpu.VMEM((tok, width), bf16),
            pltpu.VMEM((3, tok, width), bf16),
            pltpu.VMEM((tok, width), jnp.float32),
            pltpu.VMEM((4, 2, 4, tok, width + EXTRA), bf16),
            pltpu.VMEM((4, 2, 4, tok, width), bf16),
            pltpu.VMEM((4, 4, tok, width), bf16),
            pltpu.VMEM((4, 2, tok, width), bf16),
            pltpu.VMEM((4, tok, width), bf16),
            pltpu.VMEM((4, tok, width), bf16),
            dma((8,)),
            dma((3,)), dma((3,)),
            dma((5,)), dma((4,)),
            dma((4, 3)), dma((4, 3)),
            dma((4, 4)), dma((4, 4)),
            dma((4,)), dma((4,)),
            dma((4, 2)), dma((4, 2)),
            dma((4,)), dma((4,)),
            dma((3,)), dma((4,)),
        ],
        compiler_params=pltpu.CompilerParams(
            collective_id=0, has_side_effects=True, vmem_limit_bytes=60 * 1024 * 1024
        ),
        cost_estimate=pl.CostEstimate(
            flops=6 * 32 * tok * width * hidden,
            bytes_accessed=6 * width * hidden,
            transcendentals=32 * tok * hidden,
        ),
    )(
        attn_partial.reshape(-1, tok, width), residual, norm_gain.reshape(1, width),
        expert_ids.T, route_weight.T, w_gate[0], w_up[0], w_down[0],
    )


def slots_body(attn_partial, residual, norm_gain, expert_ids, route_weight, w_gate, w_up, w_down):
    width = residual.shape[1]
    tok_rows = residual.shape[0]
    top_picks = expert_ids.shape[1]
    n_expert = lax.axis_size("expert")
    n_tensor = lax.axis_size("tensor")
    experts = n_expert * n_tensor // 2
    capacity = max(2, min(tok_rows, 2 * tok_rows * top_picks // experts))
    attn_total = lax.psum_scatter(
        attn_partial[0].astype(jnp.float32).astype(jnp.bfloat16),
        "tensor",
        scatter_dimension=0,
        tiled=True,
    ).astype(jnp.float32)
    stream = residual.astype(jnp.float32) + attn_total
    scale = lax.rsqrt(jnp.mean(stream * stream, axis=-1, keepdims=True) + epsilon)
    normed = (stream * scale * norm_gain).astype(jnp.bfloat16)
    weights = route_weight.astype(jnp.float32) / 2048.0
    picked = expert_ids[None, :, :] == jnp.arange(experts, dtype=jnp.int32)[:, None, None]
    chosen = jnp.any(picked, axis=-1)
    weighting = jnp.sum(jnp.where(picked, weights[None, :, :], jnp.float32(0.0)), axis=-1)
    position = jnp.cumsum(chosen.astype(jnp.int32), axis=1) - 1
    slots = jnp.arange(capacity, dtype=jnp.int32)
    selector = chosen[:, None, :] & (position[:, None, :] == slots[None, :, None])
    gathered = jnp.einsum(
        "ect,td->ecd", selector.astype(jnp.bfloat16), normed, preferred_element_type=jnp.float32
    ).astype(jnp.bfloat16)
    outgoing = jnp.broadcast_to(gathered[:, None], (experts, 2, capacity, width))
    direct_send = outgoing.reshape(n_expert * n_tensor, capacity, width)
    incoming = lax.all_to_all(
        direct_send, ("expert", "tensor"), split_axis=0, concat_axis=0, tiled=True
    )
    flattened = incoming.reshape(-1, width)
    gate_out = jnp.dot(flattened, w_gate[0], preferred_element_type=jnp.float32)
    up_out = jnp.dot(flattened, w_up[0], preferred_element_type=jnp.float32)
    activated = (jax.nn.silu(gate_out) * up_out).astype(jnp.bfloat16)
    half_out = jnp.dot(activated, w_down[0], preferred_element_type=jnp.float32).astype(
        jnp.bfloat16
    )
    returned = lax.all_to_all(
        half_out.reshape(incoming.shape),
        ("expert", "tensor"),
        split_axis=0,
        concat_axis=0,
        tiled=True,
    )
    returned = returned.reshape(experts, 2, capacity, width)
    combined = returned[:, 0].astype(jnp.float32) + returned[:, 1].astype(jnp.float32)
    mixing = selector.astype(jnp.float32) * weighting[:, None, :]
    expert_mix = jnp.einsum("ect,ecd->td", mixing, combined, precision=lax.Precision.HIGHEST)
    return (stream + expert_mix).astype(jnp.bfloat16)


def solution(mesh):
    in_specs = (
        P("tensor", ("groups", "expert"), None),
        P(("groups", "expert", "tensor"), None),
        P(),
        P(("groups", "expert", "tensor"), None),
        P(("groups", "expert", "tensor"), None),
        P(("expert", "tensor"), None, None),
        P(("expert", "tensor"), None, None),
        P(("expert", "tensor"), None, None),
    )
    out_specs = P(("groups", "expert", "tensor"), None)
    dense = (mesh.shape["expert"], mesh.shape["tensor"]) == (8, 4)
    body = gather_body if dense else slots_body
    return jax.shard_map(body, mesh=mesh, in_specs=in_specs, out_specs=out_specs, check_vma=False)
```
